32 devices in a mesh: row: 8 (over z, y), col: 4 (over x, core).
Axes of the slice: x: 2, y: 2, z: 4, core: 2. Of those that a mesh axis runs over, the one named last changes fastest.
Arguments:
- sources: bfloat16 [32768, 128], P(('col', 'row')), may hold values from -6 to 6
- adjoint_sources: bfloat16 [32768, 128], P(('row', 'col')), may hold values from -6 to 6
- points: float32 [2, 32768], replicated, may hold values from 0 to 40
- element_of: int32 [32768], replicated, may hold values from 0 to 127
- wavenumbers: float32 [128], replicated, may hold values from 1.5 to 4
- quad_weight: float32 [32768], replicated, may hold values from 0.01 to 0.04
- near_leaves: int32 [8, 4, 2, 24], P('row', 'col'), may hold values from 0 to 15, as said below
- helper_slot: int32 [8, 4, 24], P('row', 'col'), may hold values from -1 to 11, as said below
- far_leaves: int32 [8, 4, 2, 32], P('row', 'col'), may hold values from 0 to 15, as said below
- far_rank: int32 [8, 4, 32], P('row', 'col'), may hold values from 16 to 64
- far_left: bfloat16 [8, 4, 32, 512, 128], P('row', 'col'), may hold values from -0.125 to 0.125
- far_right: bfloat16 [8, 4, 32, 512, 128], P('row', 'col'), may hold values from -0.1875 to 0.1875
Outputs:
- field: float32 [32768, 128], P(('row', 'col'))
- adjoint_field: float32 [32768, 128], P(('col', 'row'))
The draws below stay inside these ranges and needn't reach their ends.
Inputs may be any that keep to these rules, and one draw needn't show every extreme that they name: `near_leaves`: entry [r, c, 0, t] is a row leaf within row segment r (below 8) and entry [r, c, 1, t] a column leaf within column segment c (below 16); in one block of the partition all near and far pairs are distinct. `far_leaves`: as for near_leaves: row leaves below 8, column leaves below 16, and no pair of a block repeats a near or far pair of that block. Task slot t of block (r, c) belongs to the helper at row index t // 3 with the same col index. Within one col index, each pair (helper, helper_slot) is used by at most one task, so a helper takes at most 12 tasks; in every col index some block has all 24 slots live.
All inputs are finite; a program needn't handle non-finite values.
Results may differ from the reference program's by a relative error of at most 0.0031.
Values may be sent and summed in bfloat16 or wider, within the bound.
A program may use at most 128 MiB of HBM per device.

```python
import math
import jax
import jax.numpy as jnp
from jax import lax

LEAF = 512
NSRC = 64
RMAX = 64
NELEM = 128
SEND_MOST = 3
LR = 8
NA_DEV = 32
LC = 16
NUNK = 32768
NT_MAX = 24
HCAP = 12
N_ROW = 8
N_COL = 4


def pair_order(key):
    block_keys = jax.random.split(key, N_ROW * N_COL)
    pair_orders = jax.vmap(lambda one_key: jax.random.permutation(one_key, LR * LC))(block_keys)
    return pair_orders.reshape(N_ROW, N_COL, LR * LC).astype(jnp.int32)


def draw_near_leaves(key, part):
    pair_orders = pair_order(key)
    chosen = pair_orders[:, :, :NT_MAX]
    return jnp.stack([chosen // LC, chosen % LC], axis=2).astype(jnp.int32)


def draw_far_leaves(key, part):
    pair_orders = pair_order(key)
    chosen = pair_orders[:, :, NT_MAX:NT_MAX + NA_DEV]
    return jnp.stack([chosen // LC, chosen % LC], axis=2).astype(jnp.int32)


def draw_helper_slot(key, part):
    key = jax.random.fold_in(key, 7)
    group_keys = jax.random.split(key, N_COL)

    def one_group(group_key):
        order_key, want_key, turn_key = jax.random.split(group_key, 3)
        owner_order = jax.random.permutation(order_key, N_ROW).astype(jnp.int32)
        wanted = jax.random.randint(want_key, (N_ROW,), NT_MAX // 2, NT_MAX + 1).astype(jnp.int32)
        wanted = wanted.at[0].set(NT_MAX)
        offsets = jax.random.randint(turn_key, (N_ROW,), 0, N_ROW).astype(jnp.int32)

        def owner_step(capacity, entry):
            want_now, offset = entry
            available = jnp.minimum(capacity, SEND_MOST)
            rolled = jnp.roll(available, -offset)
            before = jnp.cumsum(rolled) - rolled
            taken = jnp.clip(want_now - before, 0, rolled)
            granted = jnp.roll(taken, offset)
            return (capacity - granted, (granted, HCAP - capacity))
        start = jnp.full((N_ROW,), HCAP, jnp.int32)
        _, (granted, first_free) = lax.scan(owner_step, start, (wanted, offsets))
        within = jnp.arange(SEND_MOST, dtype=jnp.int32)
        slot_ids = jnp.where(within[None, None, :] < granted[:, :, None], first_free[:, :, None] + within[None, None, :], -1)
        slot_ids = slot_ids.reshape(N_ROW, NT_MAX).astype(jnp.int32)
        inverse = jnp.argsort(owner_order, stable=True)
        return slot_ids[inverse]
    per_group = jax.vmap(one_group)(group_keys)
    return jnp.transpose(per_group, (1, 0, 2)).astype(jnp.int32)


def with_ends(array, rng, low, largest):
    longest = array.shape.index(max(array.shape))
    spots = []
    for shift in (0, 1):
        where = [jax.random.randint(jax.random.fold_in(rng, axis), (), 0, length) for axis, length in enumerate(array.shape)]
        where[longest] = (where[longest] + shift) % array.shape[longest]
        spots.append(tuple(where))
    return array.at[spots[0]].set(low).at[spots[1]].set(largest)


def block_levels(own_key, extent, pieces, least, high):
    level, own = 1.0, jax.random.fold_in(own_key, 6)
    for axis_at, blocks in pieces:
        draws = jnp.exp(jax.random.uniform(jax.random.fold_in(own, axis_at), (blocks,), jnp.float32, least / len(pieces), high / len(pieces)))
        level = level * jnp.repeat(draws, extent[axis_at] // blocks).reshape([-1 if axis == axis_at else 1 for axis in range(len(extent))])
    return level


def scatter_about(key, shape, spread, reach, cuts=(), held_as=jnp.bfloat16):
    drawn = spread * jax.random.normal(key, shape, jnp.float32)
    if cuts:
        drawn = drawn * block_levels(key, shape, cuts, -0.22, 0.18)
    return jnp.clip(drawn, -reach, reach).astype(held_as)


def setup_inputs(seed: int = 0) -> dict:
    arg_keys = jax.random.split(jax.random.key(seed), 13)
    return {
        "sources": scatter_about(arg_keys[0], (NUNK, 2 * NSRC), 1.0, 6.0, ((0, 32),)),
        "adjoint_sources": scatter_about(arg_keys[1], (NUNK, 2 * NSRC), 1.0, 6.0, ((0, 32),)),
        "points": jnp.clip(jax.random.uniform(arg_keys[2], (2, NUNK), jnp.float32, 0.0, 40.0), 0.0, 40.0),
        "element_of": with_ends(jax.random.randint(arg_keys[3], (NUNK,), 0, NELEM), jax.random.fold_in(arg_keys[3], 1), 0, NELEM - 1).astype(jnp.int32),
        "wavenumbers": jnp.clip(jnp.exp(jax.random.uniform(arg_keys[4], (NELEM,), jnp.float32, math.log(1.5), math.log(4.0))), 1.5, 4.0),
        "quad_weight": jnp.clip(jnp.exp(jax.random.uniform(arg_keys[5], (NUNK,), jnp.float32, math.log(0.01), math.log(0.04))), 0.01, 0.04),
        "near_leaves": draw_near_leaves(jax.random.fold_in(arg_keys[12], 71), 0),
        "helper_slot": draw_helper_slot(jax.random.fold_in(arg_keys[12], 71), 0),
        "far_leaves": draw_far_leaves(jax.random.fold_in(arg_keys[12], 71), 0),
        "far_rank": with_ends(jax.random.randint(arg_keys[9], (N_ROW, N_COL, NA_DEV), RMAX // 4, RMAX + 1), jax.random.fold_in(arg_keys[9], 1), RMAX // 4, RMAX).astype(jnp.int32),
        "far_left": scatter_about(arg_keys[10], (N_ROW, N_COL, NA_DEV, LEAF, 2 * RMAX), (2 * RMAX * NA_DEV * N_COL // LR) ** -0.5, 0.125, ((0, 8), (1, 4))),
        "far_right": scatter_about(arg_keys[11], (N_ROW, N_COL, NA_DEV, LEAF, 2 * RMAX), (2 * LEAF) ** -0.5, 0.1875, ((0, 8), (1, 4))),
    }


DAMPING = 0.02
SOFTENING = 0.01

def rotate(data_panel):
    half_width = data_panel.shape[-1] // 2
    return jnp.concatenate([-data_panel[..., half_width:], data_panel[..., :half_width]], axis=-1)

def green_tile(points, element_of, wavenumbers, quad_weight, row_start, col_start):
    row_points = lax.dynamic_slice_in_dim(points, row_start, LEAF, 1)
    col_points = lax.dynamic_slice_in_dim(points, col_start, LEAF, 1)
    col_kinds = lax.dynamic_slice_in_dim(element_of, col_start, LEAF, 0)
    weights = lax.dynamic_slice_in_dim(quad_weight, col_start, LEAF, 0)
    matches = col_kinds[:, None] == jnp.arange(wavenumbers.shape[0], dtype=jnp.int32)[None, :]
    col_wave = lax.optimization_barrier(jnp.sum(jnp.where(matches, wavenumbers[None, :], 0.0), axis=1))
    delta_x = row_points[0][:, None] - col_points[0][None, :]
    delta_y = row_points[1][:, None] - col_points[1][None, :]
    radius_sq = delta_x * delta_x + delta_y * delta_y
    radius = jnp.sqrt(radius_sq)
    amplitude = weights[None, :] * jnp.exp(-DAMPING * radius) * (radius_sq + SOFTENING) ** (-0.25)
    phase_arg = col_wave[None, :] * radius
    return jnp.concatenate([amplitude * jnp.cos(phase_arg), amplitude * jnp.sin(phase_arg)], axis=1).astype(jnp.bfloat16)

def add_rows(target, start, values):
    current = lax.dynamic_slice_in_dim(target, start, LEAF, 0)
    return lax.dynamic_update_slice_in_dim(target, current + values, start, 0)

def reference(sources, adjoint_sources, points, element_of, wavenumbers, quad_weight, near_leaves, helper_slot, far_leaves, far_rank, far_left, far_right):
    row_base = jnp.arange(N_ROW, dtype=jnp.int32)[:, None, None] * LR
    col_base = jnp.arange(N_COL, dtype=jnp.int32)[None, :, None] * LC
    near_rows = (row_base + near_leaves[:, :, 0, :]).reshape(-1).astype(jnp.int32)
    near_cols = (col_base + near_leaves[:, :, 1, :]).reshape(-1).astype(jnp.int32)
    near_live = (helper_slot >= 0).reshape(-1)
    far_rows = (row_base + far_leaves[:, :, 0, :]).reshape(-1).astype(jnp.int32)
    far_cols = (col_base + far_leaves[:, :, 1, :]).reshape(-1).astype(jnp.int32)
    block_ranks = far_rank.reshape(-1)
    left_all = far_left.reshape(-1, LEAF, 2 * RMAX)
    right_all = far_right.reshape(-1, LEAF, 2 * RMAX)
    field_sum = jnp.zeros(sources.shape, jnp.float32)
    adjoint_sum = jnp.zeros(sources.shape, jnp.float32)

    def near_step(state_pair, task_entry):
        row_leaf, col_leaf, is_live = task_entry

        def apply_task(sum_pair):
            field_now, adjoint_now = sum_pair
            row_start = (row_leaf * LEAF).astype(jnp.int32)
            col_start = (col_leaf * LEAF).astype(jnp.int32)
            kernel_tile = green_tile(points, element_of, wavenumbers, quad_weight, row_start, col_start)
            source = lax.dynamic_slice_in_dim(sources, col_start, LEAF, 0)
            adjoint_panel = lax.dynamic_slice_in_dim(adjoint_sources, row_start, LEAF, 0)
            forward = jnp.dot(kernel_tile, jnp.concatenate([source, rotate(source)], axis=0), preferred_element_type=jnp.float32).astype(jnp.bfloat16)
            forward = lax.optimization_barrier(forward).astype(jnp.float32)
            backward = jnp.dot(kernel_tile.T, adjoint_panel, preferred_element_type=jnp.float32)
            backward = backward[:LEAF] - rotate(backward[LEAF:])
            return (add_rows(field_now, row_start, forward), add_rows(adjoint_now, col_start, backward))
        return (lax.cond(is_live, apply_task, lambda sum_pair: sum_pair, state_pair), None)
    state_pair, _ = lax.scan(near_step, (field_sum, adjoint_sum), (near_rows, near_cols, near_live))

    def far_step(sum_pair, block_entry):
        row_leaf, col_leaf, block_rank, left_factor, right_factor = block_entry
        field_now, adjoint_now = sum_pair
        row_start = (row_leaf * LEAF).astype(jnp.int32)
        col_start = (col_leaf * LEAF).astype(jnp.int32)
        kept_rank = jnp.arange(RMAX, dtype=jnp.int32) < block_rank
        source = lax.dynamic_slice_in_dim(sources, col_start, LEAF, 0)
        adjoint_panel = lax.dynamic_slice_in_dim(adjoint_sources, row_start, LEAF, 0)
        projected = jnp.dot(right_factor.T, source, preferred_element_type=jnp.float32)
        core_block = projected[:RMAX] + rotate(projected[RMAX:])
        core_block = jnp.where(kept_rank[:, None], core_block, 0.0).astype(jnp.bfloat16)
        forward = jnp.dot(left_factor, jnp.concatenate([core_block, rotate(core_block)], axis=0), preferred_element_type=jnp.float32)
        projected = jnp.dot(left_factor.T, adjoint_panel, preferred_element_type=jnp.float32)
        adjoint_core = projected[:RMAX] - rotate(projected[RMAX:])
        adjoint_core = jnp.where(kept_rank[:, None], adjoint_core, 0.0).astype(jnp.bfloat16)
        backward = jnp.dot(right_factor, jnp.concatenate([adjoint_core, -rotate(adjoint_core)], axis=0), preferred_element_type=jnp.float32)
        return ((add_rows(field_now, row_start, forward), add_rows(adjoint_now, col_start, backward)), None)
    state_pair, _ = lax.scan(far_step, state_pair, (far_rows, far_cols, block_ranks, left_all, right_all))
    return (state_pair[0], state_pair[1])
```

```python
import math

import jax
import jax.numpy as jnp
from jax import lax
from jax.experimental import pallas as pl
from jax.experimental.pallas import tpu as pltpu
from jax.sharding import PartitionSpec as P

LEAF = 512
RMAX = 64
LANES = 128
CHUNK = 64

DAMPING = 0.02
SOFTENING = 0.01

SIN_TERMS = (4.4428679821848505, -7.307445410211019, 3.5948020760296724, -0.7844035523165803)
COS_TERMS = (
    1.4142134965678808,
    -6.978850988354271,
    5.7394611717976725,
    -1.8835629903422064,
    0.31069819203200194,
)
ROUNDER = 12582912.0


def polynomial(terms, value):
    total = terms[-1]
    for term in terms[-2::-1]:
        total = total * value + term
    return total


def rotate(panel):
    half = panel.shape[-1] // 2
    return jnp.concatenate([-panel[..., half:], panel[..., :half]], axis=-1)


def rotate_rows(panel):
    half = panel.shape[-2] // 2
    return jnp.concatenate([-panel[..., half:, :], panel[..., :half, :]], axis=-2)


def params():
    return pltpu.CompilerParams(vmem_limit_bytes=52 * 1024 * 1024)


def tile_kernel(rows_ref, cols_ref, live_ref, row_points, col_info, tile_ref):
    task = pl.program_id(0)

    @pl.when(live_ref[task] > 0)
    def _():
        for lane in range(LEAF // LANES):
            span = slice(lane * LANES, (lane + 1) * LANES)
            col_x = col_info[0, 0:1, span]
            col_y = col_info[0, 1:2, span]
            col_turns = col_info[0, 2:3, span]
            col_weight = col_info[0, 3:4, span]

            def chunk(step, carry):
                rows = pl.ds(pl.multiple_of(step * CHUNK, CHUNK), CHUNK)
                delta_x = row_points[0, 0, rows, :] - col_x
                delta_y = row_points[1, 0, rows, :] - col_y
                radius_sq = delta_x * delta_x + delta_y * delta_y
                radius = radius_sq * lax.rsqrt(jnp.maximum(radius_sq, 1e-30))
                softened = radius_sq + SOFTENING
                fourth = lax.rsqrt(softened * lax.rsqrt(softened))
                decay = jnp.exp2(radius * (-DAMPING * math.log2(math.e)))
                amplitude = (col_weight * decay) * fourth
                turns = radius * col_turns
                part = turns - ((turns + ROUNDER) - ROUNDER)
                part_sq = part * part
                sine = part * polynomial(SIN_TERMS, part_sq)
                cosine = polynomial(COS_TERMS, part_sq)
                scaled = amplitude * sine
                tile_ref[0, 0, rows, span] = (amplitude - scaled * sine).astype(jnp.bfloat16)
                tile_ref[0, 1, rows, span] = (scaled * cosine).astype(jnp.bfloat16)
                return carry

            lax.fori_loop(0, LEAF // CHUNK, chunk, 0)


def make_tiles(near_rows, near_cols, live, row_points, col_info):
    count = near_rows.shape[0]
    return pl.pallas_call(
        tile_kernel,
        out_shape=jax.ShapeDtypeStruct((count, 2, LEAF, LEAF), jnp.bfloat16),
        grid_spec=pltpu.PrefetchScalarGridSpec(
            num_scalar_prefetch=3,
            grid=(count,),
            in_specs=[
                pl.BlockSpec((2, 1, LEAF, LANES), lambda t, r, c, v: (0, r[t], 0, 0)),
                pl.BlockSpec((1, 8, LEAF), lambda t, r, c, v: (c[t], 0, 0)),
            ],
            out_specs=pl.BlockSpec((1, 2, LEAF, LEAF), lambda t, r, c, v: (t, 0, 0, 0)),
        ),
        compiler_params=params(),
        cost_estimate=pl.CostEstimate(
            flops=60 * count * LEAF * LEAF * 100, bytes_accessed=count * 4 * LEAF * LEAF, transcendentals=0
        ),
        name="tiles",
    )(near_rows, near_cols, live, row_points, col_info)


def dot(left, right, left_dim, right_dim):
    return lax.dot_general(
        left, right, (((left_dim,), (right_dim,)), ((), ())), preferred_element_type=jnp.float32
    )


def core_of(projected, rank, sign):
    swapped = rotate_rows(projected[:, RMAX:])
    core = projected[:, :RMAX] + sign * swapped
    kept = lax.broadcasted_iota(jnp.int32, core.shape, 1) < rank
    core = jnp.where(kept, core, 0.0)
    both = jnp.concatenate([core, sign * rotate_rows(core)], axis=1)
    return both.astype(jnp.bfloat16)


def adjoint_kernel(
    per_step, nr, nc, live, fr, fc, rank, tiles, panel, turned, left, right, total, narrow
):
    step = pl.program_id(0)
    near_per, far_per = per_step

    @pl.when(step == 0)
    def _():
        total[...] = jnp.zeros_like(total)

    for local in range(near_per):
        task = step * near_per + local

        @pl.when(live[task] > 0)
        def _():
            row = nr[task]
            col = nc[task]
            total[col] += dot(panel[row], tiles[local, 0], 1, 0) + dot(
                turned[row], tiles[local, 1], 1, 0
            )

    for local in range(far_per):
        block = step * far_per + local
        row = fr[block]
        col = fc[block]
        projected = dot(panel[row], left[local], 1, 0)
        core = core_of(projected, rank[block], -1.0)
        total[col] += dot(core, right[local], 1, 1)

    @pl.when(step == pl.num_programs(0) - 1)
    def _():
        narrow[...] = total[...].astype(jnp.bfloat16)


def forward_kernel(
    per_step, nr, nc, live, fr, fc, rank, tiles, source, turned, source_t, left, right, total, narrow
):
    step = pl.program_id(0)
    near_per, far_per = per_step

    @pl.when(step == 0)
    def _():
        total[...] = jnp.zeros_like(total)

    for local in range(near_per):
        task = step * near_per + local

        @pl.when(live[task] > 0)
        def _():
            row = nr[task]
            col = nc[task]
            product = dot(tiles[local, 0], source[col], 1, 0) + dot(
                tiles[local, 1], turned[col], 1, 0
            )
            total[row] += product.astype(jnp.bfloat16).astype(jnp.float32)

    for local in range(far_per):
        block = step * far_per + local
        row = fr[block]
        col = fc[block]
        projected = dot(source_t[col], right[local], 1, 0)
        core = core_of(projected, rank[block], 1.0)
        total[row] += dot(left[local], core, 1, 1)

    @pl.when(step == pl.num_programs(0) - 1)
    def _():
        narrow[...] = total[...].astype(jnp.bfloat16)


def apply_blocks(kernel, name, lists, tiles, panels, left, right, out_shape):
    near_count = tiles.shape[0]
    far_count = left.shape[0]
    steps = math.gcd(near_count, far_count)
    near_per, far_per = near_count // steps, far_count // steps

    def whole(shape):
        zeros = (0,) * len(shape)
        return pl.BlockSpec(shape, lambda t, *_: zeros)

    factor = pl.BlockSpec((far_per, LEAF, 2 * RMAX), lambda t, *_: (t, 0, 0))

    def body(*refs):
        kernel((near_per, far_per), *refs)

    return pl.pallas_call(
        body,
        out_shape=(
            jax.ShapeDtypeStruct(out_shape, jnp.float32),
            jax.ShapeDtypeStruct(out_shape, jnp.bfloat16),
        ),
        grid_spec=pltpu.PrefetchScalarGridSpec(
            num_scalar_prefetch=6,
            grid=(steps,),
            in_specs=[
                pl.BlockSpec((near_per, 2, LEAF, LEAF), lambda t, *_: (t, 0, 0, 0)),
                *[whole(panel.shape) for panel in panels],
                factor,
                factor,
            ],
            out_specs=(whole(out_shape), whole(out_shape)),
        ),
        compiler_params=params(),
        cost_estimate=pl.CostEstimate(
            flops=near_count * 4 * LEAF * LEAF * LANES * 30, bytes_accessed=near_count * 4 * LEAF * LEAF, transcendentals=0
        ),
        name=name,
    )(*lists, tiles, *panels, left, right)


def scatter_sum(wide, narrow, axis, index, size):
    unit = (wide.shape[0] * wide.shape[1]) // size
    wide = wide.reshape((size, unit) + wide.shape[2:])
    narrow = narrow.reshape((size, unit) + narrow.shape[2:])
    own = lax.dynamic_index_in_dim(wide, index, 0, keepdims=False)
    arrived = []
    for shift in range(1, size):
        target = lax.rem(index + shift, size)
        piece = lax.dynamic_index_in_dim(narrow, target, 0, keepdims=False)
        arrived.append(
            lax.ppermute(piece, axis, [(at, (at + shift) % size) for at in range(size)])
        )
    for piece in arrived:
        own = own + piece.astype(jnp.float32)
    return own


def make_per_device(row_size, col_size):
    def per_device(
        sources,
        adjoint_sources,
        points,
        element_of,
        wavenumbers,
        quad_weight,
        near_leaves,
        helper_slot,
        far_leaves,
        far_rank,
        far_left,
        far_right,
    ):
        row_index = lax.axis_index("row")
        col_index = lax.axis_index("col")
        width = sources.shape[1]
        source_block = lax.all_gather(sources, "row", axis=0, tiled=True)
        adjoint_block = lax.all_gather(adjoint_sources, "col", axis=0, tiled=True)
        col_count = source_block.shape[0] // LEAF
        row_count = adjoint_block.shape[0] // LEAF
        near_rows = near_leaves[0, 0, 0]
        near_cols = near_leaves[0, 0, 1]
        live = (helper_slot[0, 0] >= 0).astype(jnp.int32)
        far_rows = far_leaves[0, 0, 0]
        far_cols = far_leaves[0, 0, 1]
        ranks = far_rank[0, 0]
        left = far_left[0, 0]
        right = far_right[0, 0]

        row_span = row_count * LEAF
        col_span = col_count * LEAF
        row_points = lax.dynamic_slice_in_dim(points, row_index * row_span, row_span, 1)
        row_points = jnp.broadcast_to(
            row_points.reshape(2, row_count, LEAF, 1), (2, row_count, LEAF, LANES)
        )
        col_points = lax.dynamic_slice_in_dim(points, col_index * col_span, col_span, 1)
        kinds = lax.dynamic_slice_in_dim(element_of, col_index * col_span, col_span, 0)
        weights = lax.dynamic_slice_in_dim(quad_weight, col_index * col_span, col_span, 0)
        matches = jnp.arange(wavenumbers.shape[0], dtype=jnp.int32)[:, None] == kinds[None, :]
        turns = jnp.sum(
            jnp.where(matches, (wavenumbers * (0.5 / math.pi))[:, None], 0.0), axis=0
        )
        nothing = jnp.zeros_like(turns)
        col_info = jnp.stack(
            [col_points[0], col_points[1], turns, weights, nothing, nothing, nothing, nothing]
        )
        col_info = col_info.reshape(8, col_count, LEAF).transpose(1, 0, 2)
        tiles = make_tiles(near_rows, near_cols, live, row_points, col_info)

        lists = (near_rows, near_cols, live, far_rows, far_cols, ranks)
        panel = adjoint_block.reshape(row_count, LEAF, width).transpose(0, 2, 1)
        adjoint_wide, adjoint_narrow = apply_blocks(
            adjoint_kernel,
            "adjoint",
            lists,
            tiles,
            (panel, -rotate_rows(panel)),
            left,
            right,
            (col_count, width, LEAF),
        )
        adjoint_narrow, tiles = lax.optimization_barrier((adjoint_narrow, tiles))

        source = source_block.reshape(col_count, LEAF, width)
        field_wide, field_narrow = apply_blocks(
            forward_kernel,
            "forward",
            lists,
            tiles,
            (source, rotate(source), source.transpose(0, 2, 1)),
            left,
            right,
            (row_count, LEAF, width),
        )

        unit = col_span // row_size
        if unit % LEAF == 0:
            adjoint = scatter_sum(
                adjoint_wide.reshape(row_size, -1, width, LEAF),
                adjoint_narrow.reshape(row_size, -1, width, LEAF),
                "row",
                row_index,
                row_size,
            )
            adjoint_field = adjoint.transpose(0, 2, 1).reshape(unit, width)
        else:
            adjoint = scatter_sum(
                adjoint_wide.transpose(0, 2, 1).reshape(row_size, unit, width),
                adjoint_narrow.transpose(0, 2, 1).reshape(row_size, unit, width),
                "row",
                row_index,
                row_size,
            )
            adjoint_field = adjoint.reshape(unit, width)
        unit = row_span // col_size
        field = scatter_sum(
            field_wide.reshape(col_size, unit, width),
            field_narrow.reshape(col_size, unit, width),
            "col",
            col_index,
            col_size,
        )
        return (field.reshape(unit, width), adjoint_field)

    return per_device


def solution(mesh):
    return jax.shard_map(
        make_per_device(mesh.shape["row"], mesh.shape["col"]),
        mesh=mesh,
        in_specs=(
            P(("col", "row"), None),
            P(("row", "col"), None),
            P(),
            P(),
            P(),
            P(),
            P("row", "col", None, None),
            P("row", "col", None),
            P("row", "col", None, None),
            P("row", "col", None),
            P("row", "col", None, None, None),
            P("row", "col", None, None, None),
        ),
        out_specs=(P(("row", "col"), None), P(("col", "row"), None)),
        check_vma=False,
    )
```

```python
import math

import jax
import jax.numpy as jnp
from jax import lax
from jax.experimental import pallas as pl
from jax.experimental.pallas import tpu as pltpu
from jax.sharding import PartitionSpec as P

LEAF = 512
RMAX = 64
LANES = 128
CHUNK = 64

DAMPING = 0.02
SOFTENING = 0.01

SIN_TERMS = (4.4428679821848505, -7.307445410211019, 3.5948020760296724, -0.7844035523165803)
COS_TERMS = (
    1.4142134965678808,
    -6.978850988354271,
    5.7394611717976725,
    -1.8835629903422064,
    0.31069819203200194,
)
ROUNDER = 12582912.0


def polynomial(terms, value):
    total = terms[-1]
    for term in terms[-2::-1]:
        total = total * value + term
    return total


def rotate(panel):
    half = panel.shape[-1] // 2
    return jnp.concatenate([-panel[..., half:], panel[..., :half]], axis=-1)


def rotate_rows(panel):
    half = panel.shape[-2] // 2
    return jnp.concatenate([-panel[..., half:, :], panel[..., :half, :]], axis=-2)


def params():
    return pltpu.CompilerParams(vmem_limit_bytes=52 * 1024 * 1024)


def tile_kernel(
    rows_ref,
    cols_ref,
    live_ref,
    place_ref,
    row_points,
    col_points,
    kinds,
    weights,
    waves,
    tile_ref,
    row_wide,
    col_info,
):
    task = pl.program_id(0)

    @pl.when(task == 0)
    def _():
        def widen(leaf, carry):
            span = pl.ds(pl.multiple_of(leaf * LEAF, LEAF), LEAF)
            for axis in range(2):
                line = row_points[axis : axis + 1, span]
                row_wide[axis, leaf] = jnp.broadcast_to(line, (LANES, LEAF)).T
            return carry

        lax.fori_loop(0, row_wide.shape[1], widen, 0)

        def gather(leaf, carry):
            span = pl.ds(pl.multiple_of(leaf * LEAF, LEAF), LEAF)
            count = waves.shape[0]
            ids = lax.broadcasted_iota(jnp.int32, (count, LEAF), 0)
            chosen = jnp.where(ids == kinds[:, span], waves[...], 0.0)
            col_info[leaf, 0:1] = col_points[0:1, span]
            col_info[leaf, 1:2] = col_points[1:2, span]
            col_info[leaf, 2:3] = jnp.sum(chosen, axis=0, keepdims=True)
            col_info[leaf, 3:4] = weights[:, span]
            return carry

        lax.fori_loop(0, col_info.shape[0], gather, 0)

    @pl.when(live_ref[task] > 0)
    def _():
        row = rows_ref[task]
        col = cols_ref[task]
        for lane in range(LEAF // LANES):
            span = slice(lane * LANES, (lane + 1) * LANES)
            col_x = col_info[col, 0:1, span]
            col_y = col_info[col, 1:2, span]
            col_turns = col_info[col, 2:3, span]
            col_weight = col_info[col, 3:4, span]

            def chunk(step, carry):
                rows = pl.ds(pl.multiple_of(step * CHUNK, CHUNK), CHUNK)
                delta_x = row_wide[0, row, rows, :] - col_x
                delta_y = row_wide[1, row, rows, :] - col_y
                radius_sq = delta_x * delta_x + delta_y * delta_y
                radius = radius_sq * lax.rsqrt(jnp.maximum(radius_sq, 1e-30))
                softened = radius_sq + SOFTENING
                fourth = lax.rsqrt(softened * lax.rsqrt(softened))
                decay = jnp.exp2(radius * (-DAMPING * math.log2(math.e)))
                amplitude = (col_weight * decay) * fourth
                turns = radius * col_turns
                part = turns - ((turns + ROUNDER) - ROUNDER)
                part_sq = part * part
                sine = part * polynomial(SIN_TERMS, part_sq)
                cosine = polynomial(COS_TERMS, part_sq)
                scaled = amplitude * sine
                tile_ref[0, 0, rows, span] = (amplitude - scaled * sine).astype(jnp.bfloat16)
                tile_ref[0, 1, rows, span] = (scaled * cosine).astype(jnp.bfloat16)
                return carry

            lax.fori_loop(0, LEAF // CHUNK, chunk, 0)


def make_tiles(near_rows, near_cols, live, place, points, kinds, weights, waves, row_count, col_count):
    count = near_rows.shape[0]
    return pl.pallas_call(
        tile_kernel,
        out_shape=jax.ShapeDtypeStruct((count, 2, LEAF, LEAF), jnp.bfloat16),
        grid_spec=pltpu.PrefetchScalarGridSpec(
            num_scalar_prefetch=4,
            grid=(count,),
            in_specs=[
                pl.BlockSpec((2, row_count * LEAF), lambda t, r, c, v, p: (0, p[0])),
                pl.BlockSpec((2, col_count * LEAF), lambda t, r, c, v, p: (0, p[1])),
                pl.BlockSpec((1, col_count * LEAF), lambda t, r, c, v, p: (0, p[1])),
                pl.BlockSpec((1, col_count * LEAF), lambda t, r, c, v, p: (0, p[1])),
                pl.BlockSpec(waves.shape, lambda t, r, c, v, p: (0, 0)),
            ],
            out_specs=pl.BlockSpec((1, 2, LEAF, LEAF), lambda t, r, c, v, p: (t, 0, 0, 0)),
            scratch_shapes=[
                pltpu.VMEM((2, row_count, LEAF, LANES), jnp.float32),
                pltpu.VMEM((col_count, 8, LEAF), jnp.float32),
            ],
        ),
        compiler_params=params(),
        cost_estimate=pl.CostEstimate(
            flops=60 * count * LEAF * LEAF * 100, bytes_accessed=count * 4 * LEAF * LEAF, transcendentals=0
        ),
        name="tiles",
    )(near_rows, near_cols, live, place, points, points, kinds, weights, waves)


def dot(left, right, left_dim, right_dim):
    return lax.dot_general(
        left, right, (((left_dim,), (right_dim,)), ((), ())), preferred_element_type=jnp.float32
    )


def core_of(projected, rank, sign):
    swapped = rotate_rows(projected[:, RMAX:])
    core = projected[:, :RMAX] + sign * swapped
    kept = lax.broadcasted_iota(jnp.int32, core.shape, 1) < rank
    core = jnp.where(kept, core, 0.0)
    both = jnp.concatenate([core, sign * rotate_rows(core)], axis=1)
    return both.astype(jnp.bfloat16)


def adjoint_kernel(
    per_step, nr, nc, live, fr, fc, rank, place, tiles, left, right, *rest
):
    *pieces, total, narrow, panel, turned = rest
    step = pl.program_id(0)
    near_per, far_per = per_step

    @pl.when(step == 0)
    def _():
        total[...] = jnp.zeros_like(total)
        leaves = pieces[0].shape[0] // LEAF
        for shift, piece in enumerate(pieces):
            owner = lax.rem(place[1] - shift + len(pieces), len(pieces))
            for local in range(leaves):
                flipped = piece[local * LEAF : (local + 1) * LEAF, :].T
                panel[owner * leaves + local] = flipped
                turned[owner * leaves + local] = -rotate_rows(flipped)

    blocks = [step * far_per + local for local in range(far_per)]
    projected = [dot(panel[fr[b]], left[n], 1, 0) for n, b in enumerate(blocks)]
    tasks = [step * near_per + local for local in range(near_per)]
    near = [
        dot(panel[nr[t]], tiles[n, 0], 1, 0) + dot(turned[nr[t]], tiles[n, 1], 1, 0)
        for n, t in enumerate(tasks)
    ]
    cores = [core_of(projected[n], rank[b], -1.0) for n, b in enumerate(blocks)]
    for n, t in enumerate(tasks):
        total[nc[t]] += jnp.where(live[t] > 0, near[n], 0.0)
    for n, b in enumerate(blocks):
        total[fc[b]] += dot(cores[n], right[n], 1, 1)

    @pl.when(step == pl.num_programs(0) - 1)
    def _():
        narrow[...] = total[...].astype(jnp.bfloat16)


def forward_kernel(
    per_step, nr, nc, live, fr, fc, rank, place, tiles, left, right, source, total, narrow, flat, turned
):
    step = pl.program_id(0)
    near_per, far_per = per_step

    @pl.when(step == 0)
    def _():
        total[...] = jnp.zeros_like(total)

        def prepare(leaf, carry):
            block = source[leaf]
            flat[leaf] = block.T
            turned[leaf] = rotate(block)
            return carry

        lax.fori_loop(0, source.shape[0], prepare, 0)

    blocks = [step * far_per + local for local in range(far_per)]
    projected = [dot(flat[fc[b]], right[n], 1, 0) for n, b in enumerate(blocks)]
    tasks = [step * near_per + local for local in range(near_per)]
    near = [
        dot(tiles[n, 0], source[nc[t]], 1, 0) + dot(tiles[n, 1], turned[nc[t]], 1, 0)
        for n, t in enumerate(tasks)
    ]
    cores = [core_of(projected[n], rank[b], 1.0) for n, b in enumerate(blocks)]
    for n, t in enumerate(tasks):
        product = near[n].astype(jnp.bfloat16).astype(jnp.float32)
        total[nr[t]] += jnp.where(live[t] > 0, product, 0.0)
    for n, b in enumerate(blocks):
        total[fr[b]] += dot(left[n], cores[n], 1, 1)

    @pl.when(step == pl.num_programs(0) - 1)
    def _():
        narrow[...] = total[...].astype(jnp.bfloat16)


def apply_blocks(kernel, name, lists, tiles, panels, left, right, out_shape, scratch):
    near_count = tiles.shape[0]
    far_count = left.shape[0]
    steps = math.gcd(near_count, far_count)
    near_per, far_per = near_count // steps, far_count // steps

    def whole(shape):
        zeros = (0,) * len(shape)
        return pl.BlockSpec(shape, lambda t, *_: zeros)

    factor = pl.BlockSpec((far_per, LEAF, 2 * RMAX), lambda t, *_: (t, 0, 0))

    def body(*refs):
        kernel((near_per, far_per), *refs)

    return pl.pallas_call(
        body,
        out_shape=(
            jax.ShapeDtypeStruct(out_shape, jnp.float32),
            jax.ShapeDtypeStruct(out_shape, jnp.bfloat16),
        ),
        grid_spec=pltpu.PrefetchScalarGridSpec(
            num_scalar_prefetch=7,
            grid=(steps,),
            in_specs=[
                pl.BlockSpec((near_per, 2, LEAF, LEAF), lambda t, *_: (t, 0, 0, 0)),
                factor,
                factor,
                *[whole(panel.shape) for panel in panels],
            ],
            out_specs=(whole(out_shape), whole(out_shape)),
            scratch_shapes=[pltpu.VMEM(shape, jnp.bfloat16) for shape in scratch],
        ),
        compiler_params=params(),
        cost_estimate=pl.CostEstimate(
            flops=near_count * 4 * LEAF * LEAF * LANES * 30, bytes_accessed=near_count * 4 * LEAF * LEAF, transcendentals=0
        ),
        name=name,
    )(*lists, tiles, left, right, *panels)


def scatter_sum(wide, narrow, axis, index, size):
    unit = (wide.shape[0] * wide.shape[1]) // size
    wide = wide.reshape((size, unit) + wide.shape[2:])
    narrow = narrow.reshape((size, unit) + narrow.shape[2:])
    own = lax.dynamic_index_in_dim(wide, index, 0, keepdims=False)
    arrived = []
    for shift in range(1, size):
        target = lax.rem(index + shift, size)
        piece = lax.dynamic_index_in_dim(narrow, target, 0, keepdims=False)
        arrived.append(
            lax.ppermute(piece, axis, [(at, (at + shift) % size) for at in range(size)])
        )
    for piece in arrived:
        own = own + piece.astype(jnp.float32)
    return own


def make_per_device(row_size, col_size):
    def per_device(
        sources,
        adjoint_sources,
        points,
        element_of,
        wavenumbers,
        quad_weight,
        near_leaves,
        helper_slot,
        far_leaves,
        far_rank,
        far_left,
        far_right,
    ):
        row_index = lax.axis_index("row")
        col_index = lax.axis_index("col")
        width = sources.shape[1]
        source_block = lax.all_gather(sources, "row", axis=0, tiled=True)
        adjoint_pieces = [adjoint_sources] + [
            lax.ppermute(
                adjoint_sources, "col", [(at, (at + shift) % col_size) for at in range(col_size)]
            )
            for shift in range(1, col_size)
        ]
        col_count = source_block.shape[0] // LEAF
        row_count = adjoint_sources.shape[0] * col_size // LEAF
        near_rows = near_leaves[0, 0, 0]
        near_cols = near_leaves[0, 0, 1]
        live = (helper_slot[0, 0] >= 0).astype(jnp.int32)
        far_rows = far_leaves[0, 0, 0]
        far_cols = far_leaves[0, 0, 1]
        ranks = far_rank[0, 0]
        left = far_left[0, 0]
        right = far_right[0, 0]

        row_span = row_count * LEAF
        col_span = col_count * LEAF
        place = jnp.stack([row_index, col_index]).astype(jnp.int32)
        tiles = make_tiles(
            near_rows,
            near_cols,
            live,
            place,
            points,
            element_of[None, :],
            quad_weight[None, :],
            jnp.broadcast_to((wavenumbers * (0.5 / math.pi))[:, None], (wavenumbers.shape[0], LEAF)),
            row_count,
            col_count,
        )

        lists = (near_rows, near_cols, live, far_rows, far_cols, ranks, place)
        adjoint_wide, adjoint_narrow = apply_blocks(
            adjoint_kernel,
            "adjoint",
            lists,
            tiles,
            adjoint_pieces,
            left,
            right,
            (col_count, width, LEAF),
            [(row_count, width, LEAF)] * 2,
        )
        adjoint_narrow, tiles = lax.optimization_barrier((adjoint_narrow, tiles))

        field_wide, field_narrow = apply_blocks(
            forward_kernel,
            "forward",
            lists,
            tiles,
            (source_block.reshape(col_count, LEAF, width),),
            left,
            right,
            (row_count, LEAF, width),
            [(col_count, width, LEAF), (col_count, LEAF, width)],
        )

        unit = col_span // row_size
        if unit % LEAF == 0:
            adjoint = scatter_sum(
                adjoint_wide.reshape(row_size, -1, width, LEAF),
                adjoint_narrow.reshape(row_size, -1, width, LEAF),
                "row",
                row_index,
                row_size,
            )
            adjoint_field = adjoint.transpose(0, 2, 1).reshape(unit, width)
        else:
            adjoint = scatter_sum(
                adjoint_wide.transpose(0, 2, 1).reshape(row_size, unit, width),
                adjoint_narrow.transpose(0, 2, 1).reshape(row_size, unit, width),
                "row",
                row_index,
                row_size,
            )
            adjoint_field = adjoint.reshape(unit, width)
        unit = row_span // col_size
        field = scatter_sum(
            field_wide.reshape(col_size, unit, width),
            field_narrow.reshape(col_size, unit, width),
            "col",
            col_index,
            col_size,
        )
        return (field.reshape(unit, width), adjoint_field)

    return per_device


def solution(mesh):
    return jax.shard_map(
        make_per_device(mesh.shape["row"], mesh.shape["col"]),
        mesh=mesh,
        in_specs=(
            P(("col", "row"), None),
            P(("row", "col"), None),
            P(),
            P(),
            P(),
            P(),
            P("row", "col", None, None),
            P("row", "col", None),
            P("row", "col", None, None),
            P("row", "col", None),
            P("row", "col", None, None, None),
            P("row", "col", None, None, None),
        ),
        out_specs=(P(("row", "col"), None), P(("col", "row"), None)),
        check_vma=False,
    )
```

```python
import functools
import math

import jax
import jax.numpy as jnp
from jax import lax
from jax.experimental import pallas as pl
from jax.experimental.pallas import tpu as pltpu
from jax.sharding import PartitionSpec as P

LEAF = 512
RMAX = 64
LANES = 128
CHUNK = 64

DAMPING = 0.02
SOFTENING = 0.01

SIN_TERMS = (4.4428679821848505, -7.307445410211019, 3.5948020760296724, -0.7844035523165803)
COS_TERMS = (
    1.4142134965678808,
    -6.978850988354271,
    5.7394611717976725,
    -1.8835629903422064,
    0.31069819203200194,
)
ROUNDER = 12582912.0


def polynomial(terms, value):
    total = terms[-1]
    for term in terms[-2::-1]:
        total = total * value + term
    return total


def rotate(panel):
    half = panel.shape[-1] // 2
    return jnp.concatenate([-panel[..., half:], panel[..., :half]], axis=-1)


def rotate_rows(panel):
    half = panel.shape[-2] // 2
    return jnp.concatenate([-panel[..., half:, :], panel[..., :half, :]], axis=-2)


def params(mebibytes):
    return pltpu.CompilerParams(vmem_limit_bytes=mebibytes * 1024 * 1024)


def tile_kernel(
    rows_ref,
    cols_ref,
    live_ref,
    place_ref,
    row_points,
    col_points,
    kinds,
    weights,
    waves,
    tile_ref,
    row_wide,
    col_info,
):
    task = pl.program_id(0)

    @pl.when(task == 0)
    def _():
        def widen(leaf, carry):
            span = pl.ds(pl.multiple_of(leaf * LEAF, LEAF), LEAF)
            for axis in range(2):
                line = row_points[axis : axis + 1, span]
                row_wide[axis, leaf] = jnp.broadcast_to(line, (LANES, LEAF)).T
            return carry

        lax.fori_loop(0, row_wide.shape[1], widen, 0)

        def gather(leaf, carry):
            span = pl.ds(pl.multiple_of(leaf * LEAF, LEAF), LEAF)
            count = waves.shape[0]
            ids = lax.broadcasted_iota(jnp.int32, (count, LEAF), 0)
            chosen = jnp.where(ids == kinds[:, span], waves[...], 0.0)
            col_info[leaf, 0:1] = col_points[0:1, span]
            col_info[leaf, 1:2] = col_points[1:2, span]
            col_info[leaf, 2:3] = jnp.sum(chosen, axis=0, keepdims=True)
            col_info[leaf, 3:4] = weights[:, span]
            return carry

        lax.fori_loop(0, col_info.shape[0], gather, 0)

    @pl.when(live_ref[task] > 0)
    def _():
        row = rows_ref[task]
        col = cols_ref[task]
        for lane in range(LEAF // LANES):
            span = slice(lane * LANES, (lane + 1) * LANES)
            col_x = col_info[col, 0:1, span]
            col_y = col_info[col, 1:2, span]
            col_turns = col_info[col, 2:3, span]
            col_weight = col_info[col, 3:4, span]

            def chunk(step, carry):
                rows = pl.ds(pl.multiple_of(step * CHUNK, CHUNK), CHUNK)
                delta_x = row_wide[0, row, rows, :] - col_x
                delta_y = row_wide[1, row, rows, :] - col_y
                radius_sq = delta_x * delta_x + delta_y * delta_y
                radius = radius_sq * lax.rsqrt(jnp.maximum(radius_sq, 1e-30))
                softened = radius_sq + SOFTENING
                fourth = lax.rsqrt(softened * lax.rsqrt(softened))
                decay = jnp.exp2(radius * (-DAMPING * math.log2(math.e)))
                amplitude = (col_weight * decay) * fourth
                turns = radius * col_turns
                part = turns - ((turns + ROUNDER) - ROUNDER)
                part_sq = part * part
                sine = part * polynomial(SIN_TERMS, part_sq)
                cosine = polynomial(COS_TERMS, part_sq)
                scaled = amplitude * sine
                tile_ref[0, 0, rows, span] = (amplitude - scaled * sine).astype(jnp.bfloat16)
                tile_ref[0, 1, rows, span] = (scaled * cosine).astype(jnp.bfloat16)
                return carry

            lax.fori_loop(0, LEAF // CHUNK, chunk, 0)


def make_tiles(near_rows, near_cols, live, place, points, kinds, weights, waves, row_count, col_count):
    count = near_rows.shape[0]
    return pl.pallas_call(
        tile_kernel,
        out_shape=jax.ShapeDtypeStruct((count, 2, LEAF, LEAF), jnp.bfloat16),
        grid_spec=pltpu.PrefetchScalarGridSpec(
            num_scalar_prefetch=4,
            grid=(count,),
            in_specs=[
                pl.BlockSpec((2, row_count * LEAF), lambda t, r, c, v, p: (0, p[0])),
                pl.BlockSpec((2, col_count * LEAF), lambda t, r, c, v, p: (0, p[1])),
                pl.BlockSpec((1, col_count * LEAF), lambda t, r, c, v, p: (0, p[1])),
                pl.BlockSpec((1, col_count * LEAF), lambda t, r, c, v, p: (0, p[1])),
                pl.BlockSpec(waves.shape, lambda t, r, c, v, p: (0, 0)),
            ],
            out_specs=pl.BlockSpec((1, 2, LEAF, LEAF), lambda t, r, c, v, p: (t, 0, 0, 0)),
            scratch_shapes=[
                pltpu.VMEM((2, row_count, LEAF, LANES), jnp.float32),
                pltpu.VMEM((col_count, 8, LEAF), jnp.float32),
            ],
        ),
        compiler_params=params(60),
        cost_estimate=pl.CostEstimate(
            flops=60 * count * LEAF * LEAF * 100, bytes_accessed=count * 4 * LEAF * LEAF, transcendentals=0
        ),
        name="tiles",
    )(near_rows, near_cols, live, place, points, points, kinds, weights, waves)


def dot(left, right, left_dim, right_dim):
    return lax.dot_general(
        left, right, (((left_dim,), (right_dim,)), ((), ())), preferred_element_type=jnp.float32
    )


def core_of(projected, rank, sign):
    swapped = rotate_rows(projected[:, RMAX:])
    core = projected[:, :RMAX] + sign * swapped
    kept = lax.broadcasted_iota(jnp.int32, core.shape, 1) < rank
    core = jnp.where(kept, core, 0.0)
    both = jnp.concatenate([core, sign * rotate_rows(core)], axis=1)
    return both.astype(jnp.bfloat16)


def hand_out(total, index, own, pieces):
    size = len(pieces) + 1
    leaves = total.shape[0] // size
    for local in range(leaves):
        own[local] = total[index * leaves + local]
    for shift, piece in enumerate(pieces, 1):
        target = lax.rem(index + shift, size)
        for local in range(leaves):
            piece[local] = total[target * leaves + local].astype(jnp.bfloat16)


def adjoint_kernel(
    size, per_step, nr, nc, live, fr, fc, rank, place, tiles, left, right, *rest
):
    *rest, total, panel, turned = rest
    pieces, own, sent = rest[:size], rest[size], rest[size + 1 :]
    step = pl.program_id(0)
    near_per, far_per = per_step

    @pl.when(step == 0)
    def _():
        total[...] = jnp.zeros_like(total)
        leaves = pieces[0].shape[0] // LEAF
        for shift, piece in enumerate(pieces):
            owner = lax.rem(place[1] - shift + len(pieces), len(pieces))
            for local in range(leaves):
                flipped = piece[local * LEAF : (local + 1) * LEAF, :].T
                panel[owner * leaves + local] = flipped
                turned[owner * leaves + local] = -rotate_rows(flipped)

    blocks = [step * far_per + local for local in range(far_per)]
    projected = [dot(panel[fr[b]], left[n], 1, 0) for n, b in enumerate(blocks)]
    tasks = [step * near_per + local for local in range(near_per)]
    near = [
        dot(panel[nr[t]], tiles[n, 0], 1, 0) + dot(turned[nr[t]], tiles[n, 1], 1, 0)
        for n, t in enumerate(tasks)
    ]
    cores = [core_of(projected[n], rank[b], -1.0) for n, b in enumerate(blocks)]
    for n, t in enumerate(tasks):
        total[nc[t]] += jnp.where(live[t] > 0, near[n], 0.0)
    for n, b in enumerate(blocks):
        total[fc[b]] += dot(cores[n], right[n], 1, 1)

    @pl.when(step == pl.num_programs(0) - 1)
    def _():
        hand_out(total, place[0], own, sent)


def forward_kernel(
    per_step, nr, nc, live, fr, fc, rank, place, tiles, left, right, source, own, *rest
):
    *sent, total, flat, turned = rest
    step = pl.program_id(0)
    near_per, far_per = per_step

    @pl.when(step == 0)
    def _():
        total[...] = jnp.zeros_like(total)

        def prepare(leaf, carry):
            block = source[leaf]
            flat[leaf] = block.T
            turned[leaf] = rotate(block)
            return carry

        lax.fori_loop(0, source.shape[0], prepare, 0)

    blocks = [step * far_per + local for local in range(far_per)]
    projected = [dot(flat[fc[b]], right[n], 1, 0) for n, b in enumerate(blocks)]
    tasks = [step * near_per + local for local in range(near_per)]
    near = [
        dot(tiles[n, 0], source[nc[t]], 1, 0) + dot(tiles[n, 1], turned[nc[t]], 1, 0)
        for n, t in enumerate(tasks)
    ]
    cores = [core_of(projected[n], rank[b], 1.0) for n, b in enumerate(blocks)]
    for n, t in enumerate(tasks):
        product = near[n].astype(jnp.bfloat16).astype(jnp.float32)
        total[nr[t]] += jnp.where(live[t] > 0, product, 0.0)
    for n, b in enumerate(blocks):
        total[fr[b]] += dot(left[n], cores[n], 1, 1)

    @pl.when(step == pl.num_programs(0) - 1)
    def _():
        hand_out(total, place[1], own, sent)


def apply_blocks(kernel, name, lists, tiles, panels, left, right, out_shape, size, scratch):
    near_count = tiles.shape[0]
    far_count = left.shape[0]
    steps = math.gcd(near_count, far_count)
    piece_shape = (out_shape[0] // size,) + out_shape[1:]
    near_per, far_per = near_count // steps, far_count // steps

    def whole(shape):
        zeros = (0,) * len(shape)
        return pl.BlockSpec(shape, lambda t, *_: zeros)

    factor = pl.BlockSpec((far_per, LEAF, 2 * RMAX), lambda t, *_: (t, 0, 0))

    def body(*refs):
        kernel((near_per, far_per), *refs)

    return pl.pallas_call(
        body,
        out_shape=[jax.ShapeDtypeStruct(piece_shape, jnp.float32)]
        + [jax.ShapeDtypeStruct(piece_shape, jnp.bfloat16)] * (size - 1),
        grid_spec=pltpu.PrefetchScalarGridSpec(
            num_scalar_prefetch=7,
            grid=(steps,),
            in_specs=[
                pl.BlockSpec((near_per, 2, LEAF, LEAF), lambda t, *_: (t, 0, 0, 0)),
                factor,
                factor,
                *[whole(panel.shape) for panel in panels],
            ],
            out_specs=[whole(piece_shape)] * size,
            scratch_shapes=[pltpu.VMEM(out_shape, jnp.float32)]
            + [pltpu.VMEM(shape, jnp.bfloat16) for shape in scratch],
        ),
        compiler_params=params(60),
        cost_estimate=pl.CostEstimate(
            flops=near_count * 4 * LEAF * LEAF * LANES * 30, bytes_accessed=near_count * 4 * LEAF * LEAF, transcendentals=0
        ),
        name=name,
    )(*lists, tiles, left, right, *panels)


def scatter_sum(pieces, axis):
    size = len(pieces)
    own = pieces[0]
    arrived = [
        lax.ppermute(piece, axis, [(at, (at + shift) % size) for at in range(size)])
        for shift, piece in enumerate(pieces[1:], 1)
    ]
    for piece in arrived:
        own = own + piece.astype(jnp.float32)
    return own


def make_per_device(row_size, col_size):
    def per_device(
        sources,
        adjoint_sources,
        points,
        element_of,
        wavenumbers,
        quad_weight,
        near_leaves,
        helper_slot,
        far_leaves,
        far_rank,
        far_left,
        far_right,
    ):
        row_index = lax.axis_index("row")
        col_index = lax.axis_index("col")
        width = sources.shape[1]
        source_block = lax.all_gather(sources, "row", axis=0, tiled=True)
        adjoint_pieces = [adjoint_sources] + [
            lax.ppermute(
                adjoint_sources, "col", [(at, (at + shift) % col_size) for at in range(col_size)]
            )
            for shift in range(1, col_size)
        ]
        col_count = source_block.shape[0] // LEAF
        row_count = adjoint_sources.shape[0] * col_size // LEAF
        near_rows = near_leaves[0, 0, 0]
        near_cols = near_leaves[0, 0, 1]
        live = (helper_slot[0, 0] >= 0).astype(jnp.int32)
        far_rows = far_leaves[0, 0, 0]
        far_cols = far_leaves[0, 0, 1]
        ranks = far_rank[0, 0]
        left = far_left[0, 0]
        right = far_right[0, 0]

        place = jnp.stack([row_index, col_index]).astype(jnp.int32)
        tiles = make_tiles(
            near_rows,
            near_cols,
            live,
            place,
            points,
            element_of[None, :],
            quad_weight[None, :],
            jnp.broadcast_to((wavenumbers * (0.5 / math.pi))[:, None], (wavenumbers.shape[0], LEAF)),
            row_count,
            col_count,
        )

        lists = (near_rows, near_cols, live, far_rows, far_cols, ranks, place)
        adjoint_parts = apply_blocks(
            functools.partial(adjoint_kernel, col_size),
            "adjoint",
            lists,
            tiles,
            adjoint_pieces,
            left,
            right,
            (col_count, width, LEAF),
            row_size,
            [(row_count, width, LEAF)] * 2,
        )
        adjoint_parts, tiles = lax.optimization_barrier((adjoint_parts, tiles))

        field_parts = apply_blocks(
            forward_kernel,
            "forward",
            lists,
            tiles,
            (source_block.reshape(col_count, LEAF, width),),
            left,
            right,
            (row_count, LEAF, width),
            col_size,
            [(col_count, width, LEAF), (col_count, LEAF, width)],
        )

        late = (adjoint_parts[1], adjoint_parts[-1])
        late, field_parts = lax.optimization_barrier((late, field_parts))
        adjoint_parts = [adjoint_parts[0], late[0], *adjoint_parts[2:-1], late[1]]
        adjoint = scatter_sum(adjoint_parts, "row")
        field = scatter_sum(field_parts, "col")
        return (field.reshape(-1, width), adjoint.transpose(0, 2, 1).reshape(-1, width))

    return per_device


def solution(mesh):
    return jax.shard_map(
        make_per_device(mesh.shape["row"], mesh.shape["col"]),
        mesh=mesh,
        in_specs=(
            P(("col", "row"), None),
            P(("row", "col"), None),
            P(),
            P(),
            P(),
            P(),
            P("row", "col", None, None),
            P("row", "col", None),
            P("row", "col", None, None),
            P("row", "col", None),
            P("row", "col", None, None, None),
            P("row", "col", None, None, None),
        ),
        out_specs=(P(("row", "col"), None), P(("col", "row"), None)),
        check_vma=False,
    )
```

```python
import functools
import math

import jax
import jax.numpy as jnp
from jax import lax
from jax.experimental import pallas as pl
from jax.experimental.pallas import tpu as pltpu
from jax.sharding import PartitionSpec as P

LEAF = 512
RMAX = 64
LANES = 128
CHUNK = 256

DAMPING = 0.02
SOFTENING = 0.01

SIN_TERMS = (4.4428679821848505, -7.307445410211019, 3.5948020760296724, -0.7844035523165803)
COS_TERMS = (
    1.4142134965678808,
    -6.978850988354271,
    5.7394611717976725,
    -1.8835629903422064,
    0.31069819203200194,
)
ROUNDER = 12582912.0


def polynomial(terms, value):
    total = terms[-1]
    for term in terms[-2::-1]:
        total = total * value + term
    return total


def rotate(panel):
    half = panel.shape[-1] // 2
    return jnp.concatenate([-panel[..., half:], panel[..., :half]], axis=-1)


def rotate_rows(panel):
    half = panel.shape[-2] // 2
    return jnp.concatenate([-panel[..., half:, :], panel[..., :half, :]], axis=-2)


def params(mebibytes):
    return pltpu.CompilerParams(vmem_limit_bytes=mebibytes * 1024 * 1024)


def tile_kernel(
    rows_ref,
    cols_ref,
    live_ref,
    place_ref,
    row_points,
    col_points,
    kinds,
    weights,
    waves,
    tile_ref,
    row_wide,
    col_info,
):
    task = pl.program_id(0)

    @pl.when(task == 0)
    def _():
        def widen(leaf, carry):
            span = pl.ds(pl.multiple_of(leaf * LEAF, LEAF), LEAF)
            for axis in range(2):
                line = row_points[axis : axis + 1, span]
                row_wide[axis, leaf] = jnp.broadcast_to(line, (LANES, LEAF)).T
            return carry

        lax.fori_loop(0, row_wide.shape[1], widen, 0)

        def gather(leaf, carry):
            span = pl.ds(pl.multiple_of(leaf * LEAF, LEAF), LEAF)
            count = waves.shape[0]
            ids = lax.broadcasted_iota(jnp.int32, (count, LEAF), 0)
            chosen = jnp.where(ids == kinds[:, span], waves[...], 0.0)
            col_info[leaf, 0:1] = col_points[0:1, span]
            col_info[leaf, 1:2] = col_points[1:2, span]
            col_info[leaf, 2:3] = jnp.sum(chosen, axis=0, keepdims=True)
            col_info[leaf, 3:4] = weights[:, span]
            return carry

        lax.fori_loop(0, col_info.shape[0], gather, 0)

    @pl.when(live_ref[task] > 0)
    def _():
        row = rows_ref[task]
        col = cols_ref[task]
        for lane in range(LEAF // LANES):
            span = slice(lane * LANES, (lane + 1) * LANES)
            col_x = col_info[col, 0:1, span]
            col_y = col_info[col, 1:2, span]
            col_turns = col_info[col, 2:3, span]
            col_weight = col_info[col, 3:4, span]

            def chunk(step, carry):
                rows = pl.ds(pl.multiple_of(step * CHUNK, CHUNK), CHUNK)
                delta_x = row_wide[0, row, rows, :] - col_x
                delta_y = row_wide[1, row, rows, :] - col_y
                radius_sq = delta_x * delta_x + delta_y * delta_y
                radius = radius_sq * lax.rsqrt(jnp.maximum(radius_sq, 1e-30))
                softened = radius_sq + SOFTENING
                fourth = lax.rsqrt(softened * lax.rsqrt(softened))
                decay = jnp.exp2(radius * (-DAMPING * math.log2(math.e)))
                amplitude = (col_weight * decay) * fourth
                turns = radius * col_turns
                part = turns - ((turns + ROUNDER) - ROUNDER)
                part_sq = part * part
                sine = part * polynomial(SIN_TERMS, part_sq)
                cosine = polynomial(COS_TERMS, part_sq)
                scaled = amplitude * sine
                tile_ref[0, 0, rows, span] = (amplitude - scaled * sine).astype(jnp.bfloat16)
                tile_ref[0, 1, rows, span] = (scaled * cosine).astype(jnp.bfloat16)
                return carry

            lax.fori_loop(0, LEAF // CHUNK, chunk, 0)


def make_tiles(near_rows, near_cols, live, place, points, kinds, weights, waves, row_count, col_count):
    count = near_rows.shape[0]
    return pl.pallas_call(
        tile_kernel,
        out_shape=jax.ShapeDtypeStruct((count, 2, LEAF, LEAF), jnp.bfloat16),
        grid_spec=pltpu.PrefetchScalarGridSpec(
            num_scalar_prefetch=4,
            grid=(count,),
            in_specs=[
                pl.BlockSpec((2, row_count * LEAF), lambda t, r, c, v, p: (0, p[0])),
                pl.BlockSpec((2, col_count * LEAF), lambda t, r, c, v, p: (0, p[1])),
                pl.BlockSpec((1, col_count * LEAF), lambda t, r, c, v, p: (0, p[1])),
                pl.BlockSpec((1, col_count * LEAF), lambda t, r, c, v, p: (0, p[1])),
                pl.BlockSpec(waves.shape, lambda t, r, c, v, p: (0, 0)),
            ],
            out_specs=pl.BlockSpec((1, 2, LEAF, LEAF), lambda t, r, c, v, p: (t, 0, 0, 0)),
            scratch_shapes=[
                pltpu.VMEM((2, row_count, LEAF, LANES), jnp.float32),
                pltpu.VMEM((col_count, 8, LEAF), jnp.float32),
            ],
        ),
        compiler_params=params(60),
        cost_estimate=pl.CostEstimate(
            flops=60 * count * LEAF * LEAF * 100, bytes_accessed=count * 4 * LEAF * LEAF, transcendentals=0
        ),
        name="tiles",
    )(near_rows, near_cols, live, place, points, points, kinds, weights, waves)


def dot(left, right, left_dim, right_dim):
    return lax.dot_general(
        left, right, (((left_dim,), (right_dim,)), ((), ())), preferred_element_type=jnp.float32
    )


def core_of(projected, rank, sign):
    swapped = rotate_rows(projected[:, RMAX:])
    core = projected[:, :RMAX] + sign * swapped
    kept = lax.broadcasted_iota(jnp.int32, core.shape, 1) < rank
    core = jnp.where(kept, core, 0.0)
    both = jnp.concatenate([core, sign * rotate_rows(core)], axis=1)
    return both.astype(jnp.bfloat16)


def hand_out(total, index, own, pieces):
    size = len(pieces) + 1
    leaves = total.shape[0] // size
    for local in range(leaves):
        own[local] = total[index * leaves + local]
    for shift, piece in enumerate(pieces, 1):
        target = lax.rem(index + shift, size)
        for local in range(leaves):
            piece[local] = total[target * leaves + local].astype(jnp.bfloat16)


def adjoint_kernel(
    size, per_step, nr, nc, live, fr, fc, rank, place, tiles, left, right, *rest
):
    *rest, total, panel, turned = rest
    pieces, own, sent = rest[:size], rest[size], rest[size + 1 :]
    step = pl.program_id(0)
    near_per, far_per = per_step

    @pl.when(step == 0)
    def _():
        total[...] = jnp.zeros_like(total)
        leaves = pieces[0].shape[0] // LEAF
        for shift, piece in enumerate(pieces):
            owner = lax.rem(place[1] - shift + len(pieces), len(pieces))
            for local in range(leaves):
                flipped = piece[local * LEAF : (local + 1) * LEAF, :].T
                panel[owner * leaves + local] = flipped
                turned[owner * leaves + local] = -rotate_rows(flipped)

    blocks = [step * far_per + local for local in range(far_per)]
    projected = [dot(panel[fr[b]], left[n], 1, 0) for n, b in enumerate(blocks)]
    tasks = [step * near_per + local for local in range(near_per)]
    near = [
        dot(panel[nr[t]], tiles[n, 0], 1, 0) + dot(turned[nr[t]], tiles[n, 1], 1, 0)
        for n, t in enumerate(tasks)
    ]
    cores = [core_of(projected[n], rank[b], -1.0) for n, b in enumerate(blocks)]
    for n, t in enumerate(tasks):
        total[nc[t]] += jnp.where(live[t] > 0, near[n], 0.0)
    for n, b in enumerate(blocks):
        total[fc[b]] += dot(cores[n], right[n], 1, 1)

    @pl.when(step == pl.num_programs(0) - 1)
    def _():
        hand_out(total, place[0], own, sent)


def forward_kernel(
    per_step, nr, nc, live, fr, fc, rank, place, tiles, left, right, source, own, *rest
):
    *sent, total, flat, turned = rest
    step = pl.program_id(0)
    near_per, far_per = per_step

    @pl.when(step == 0)
    def _():
        total[...] = jnp.zeros_like(total)

        def prepare(leaf, carry):
            block = source[leaf]
            flat[leaf] = block.T
            turned[leaf] = rotate(block)
            return carry

        lax.fori_loop(0, source.shape[0], prepare, 0)

    blocks = [step * far_per + local for local in range(far_per)]
    projected = [dot(flat[fc[b]], right[n], 1, 0) for n, b in enumerate(blocks)]
    tasks = [step * near_per + local for local in range(near_per)]
    near = [
        dot(tiles[n, 0], source[nc[t]], 1, 0) + dot(tiles[n, 1], turned[nc[t]], 1, 0)
        for n, t in enumerate(tasks)
    ]
    cores = [core_of(projected[n], rank[b], 1.0) for n, b in enumerate(blocks)]
    for n, t in enumerate(tasks):
        product = near[n].astype(jnp.bfloat16).astype(jnp.float32)
        total[nr[t]] += jnp.where(live[t] > 0, product, 0.0)
    for n, b in enumerate(blocks):
        total[fr[b]] += dot(left[n], cores[n], 1, 1)

    @pl.when(step == pl.num_programs(0) - 1)
    def _():
        hand_out(total, place[1], own, sent)


def apply_blocks(kernel, name, merge, lists, tiles, panels, left, right, out_shape, size, scratch):
    near_count = tiles.shape[0]
    far_count = left.shape[0]
    steps = max(1, math.gcd(near_count, far_count) // merge)
    piece_shape = (out_shape[0] // size,) + out_shape[1:]
    near_per, far_per = near_count // steps, far_count // steps

    def whole(shape):
        zeros = (0,) * len(shape)
        return pl.BlockSpec(shape, lambda t, *_: zeros)

    factor = pl.BlockSpec((far_per, LEAF, 2 * RMAX), lambda t, *_: (t, 0, 0))

    def body(*refs):
        kernel((near_per, far_per), *refs)

    return pl.pallas_call(
        body,
        out_shape=[jax.ShapeDtypeStruct(piece_shape, jnp.float32)]
        + [jax.ShapeDtypeStruct(piece_shape, jnp.bfloat16)] * (size - 1),
        grid_spec=pltpu.PrefetchScalarGridSpec(
            num_scalar_prefetch=7,
            grid=(steps,),
            in_specs=[
                pl.BlockSpec((near_per, 2, LEAF, LEAF), lambda t, *_: (t, 0, 0, 0)),
                factor,
                factor,
                *[whole(panel.shape) for panel in panels],
            ],
            out_specs=[whole(piece_shape)] * size,
            scratch_shapes=[pltpu.VMEM(out_shape, jnp.float32)]
            + [pltpu.VMEM(shape, jnp.bfloat16) for shape in scratch],
        ),
        compiler_params=params(60),
        cost_estimate=pl.CostEstimate(
            flops=near_count * 4 * LEAF * LEAF * LANES * 30, bytes_accessed=near_count * 4 * LEAF * LEAF, transcendentals=0
        ),
        name=name,
    )(*lists, tiles, left, right, *panels)


def scatter_sum(pieces, axis):
    size = len(pieces)
    own = pieces[0]
    arrived = [
        lax.ppermute(piece, axis, [(at, (at + shift) % size) for at in range(size)])
        for shift, piece in enumerate(pieces[1:], 1)
    ]
    for piece in arrived:
        own = own + piece.astype(jnp.float32)
    return own


def make_per_device(row_size, col_size):
    def per_device(
        sources,
        adjoint_sources,
        points,
        element_of,
        wavenumbers,
        quad_weight,
        near_leaves,
        helper_slot,
        far_leaves,
        far_rank,
        far_left,
        far_right,
    ):
        row_index = lax.axis_index("row")
        col_index = lax.axis_index("col")
        width = sources.shape[1]
        source_block = lax.all_gather(sources, "row", axis=0, tiled=True)
        adjoint_pieces = [adjoint_sources] + [
            lax.ppermute(
                adjoint_sources, "col", [(at, (at + shift) % col_size) for at in range(col_size)]
            )
            for shift in range(1, col_size)
        ]
        col_count = source_block.shape[0] // LEAF
        row_count = adjoint_sources.shape[0] * col_size // LEAF
        near_rows = near_leaves[0, 0, 0]
        near_cols = near_leaves[0, 0, 1]
        live = (helper_slot[0, 0] >= 0).astype(jnp.int32)
        far_rows = far_leaves[0, 0, 0]
        far_cols = far_leaves[0, 0, 1]
        ranks = far_rank[0, 0]
        left = far_left[0, 0]
        right = far_right[0, 0]

        place = jnp.stack([row_index, col_index]).astype(jnp.int32)
        tiles = make_tiles(
            near_rows,
            near_cols,
            live,
            place,
            points,
            element_of[None, :],
            quad_weight[None, :],
            jnp.broadcast_to((wavenumbers * (0.5 / math.pi))[:, None], (wavenumbers.shape[0], LEAF)),
            row_count,
            col_count,
        )

        lists = (near_rows, near_cols, live, far_rows, far_cols, ranks, place)
        adjoint_parts = apply_blocks(
            functools.partial(adjoint_kernel, col_size),
            "adjoint",
            2,
            lists,
            tiles,
            adjoint_pieces,
            left,
            right,
            (col_count, width, LEAF),
            row_size,
            [(row_count, width, LEAF)] * 2,
        )
        adjoint_parts, tiles = lax.optimization_barrier((adjoint_parts, tiles))

        field_parts = apply_blocks(
            forward_kernel,
            "forward",
            1,
            lists,
            tiles,
            (source_block.reshape(col_count, LEAF, width),),
            left,
            right,
            (row_count, LEAF, width),
            col_size,
            [(col_count, width, LEAF), (col_count, LEAF, width)],
        )

        late = (adjoint_parts[1], adjoint_parts[-1])
        late, field_parts = lax.optimization_barrier((late, field_parts))
        adjoint_parts = [adjoint_parts[0], late[0], *adjoint_parts[2:-1], late[1]]
        adjoint = scatter_sum(adjoint_parts, "row")
        field = scatter_sum(field_parts, "col")
        return (field.reshape(-1, width), adjoint.transpose(0, 2, 1).reshape(-1, width))

    return per_device


def solution(mesh):
    return jax.shard_map(
        make_per_device(mesh.shape["row"], mesh.shape["col"]),
        mesh=mesh,
        in_specs=(
            P(("col", "row"), None),
            P(("row", "col"), None),
            P(),
            P(),
            P(),
            P(),
            P("row", "col", None, None),
            P("row", "col", None),
            P("row", "col", None, None),
            P("row", "col", None),
            P("row", "col", None, None, None),
            P("row", "col", None, None, None),
        ),
        out_specs=(P(("row", "col"), None), P(("col", "row"), None)),
        check_vma=False,
    )
```
